32 devices in a mesh: col: 4 (over y, x), row: 8 (over z, core).
Axes of the slice: x: 2, y: 2, z: 4, core: 2. Of those that a mesh axis runs over, the one named last changes fastest.
Arguments:
- density: float32 [8, 512, 1024], P(None, 'row', 'col'), may hold values from 1 to 2
- velocity: float32 [3, 8, 512, 1024], P(None, None, 'row', 'col'), may hold values from -0.3 to 0.3
- pressure: float32 [8, 512, 1024], P(None, 'row', 'col'), may hold values from 1 to 2
Outputs:
- density_out: float32 [8, 512, 1024], P(None, 'row', 'col')
- velocity_out: float32 [3, 8, 512, 1024], P(None, None, 'row', 'col')
- pressure_out: float32 [8, 512, 1024], P(None, 'row', 'col')
The draws below stay inside these ranges and needn't reach their ends.
All inputs are finite; a program needn't handle non-finite values.
Results may differ from the reference program's by a relative error of at most 0.00002.
Values sent between devices are 32-bit elements; how exact they have to be, the bound alone decides.
A program may use at most 128 MiB of HBM per device.

```python
import math
import jax
import jax.numpy as jnp
from jax import lax

PLANES = 8
LENGTH_Y = 512
LENGTH_Z = 1024


def shard_levels(stream_key, shape, cuts, least, largest):
    level = 1.0
    for position, shards_of in cuts:
        heights = jax.random.uniform(jax.random.fold_in(jax.random.fold_in(stream_key, 6), position), (shards_of,), jnp.float32, least / len(cuts), largest / len(cuts))
        level = level * jnp.repeat(jnp.exp(heights), shape[position] // shards_of).reshape((-1,) + (1,) * (len(shape) - 1 - position))
    return level


def setup_inputs(seed: int = 0) -> dict:
    splits = jax.random.split(jax.random.key(seed), 4)
    density = jnp.clip(jnp.exp(math.log(2.0) - 0.6931472 * jax.random.uniform(splits[0], (PLANES, LENGTH_Y, LENGTH_Z), jnp.float32) ** shard_levels(splits[0], (PLANES, LENGTH_Y, LENGTH_Z), ((1, 8), (2, 4)), -0.2, 0.2)), 1.0, 2.0)
    velocity = jnp.clip(jax.random.uniform(splits[1], (3, PLANES, LENGTH_Y, LENGTH_Z), jnp.float32, -0.3, 0.3) * shard_levels(splits[1], (3, PLANES, LENGTH_Y, LENGTH_Z), ((2, 8), (3, 4)), -0.4, 0.0), -0.3, 0.3)
    pressure = jnp.clip(jnp.exp(math.log(2.0) - 0.6931472 * jax.random.uniform(splits[2], (PLANES, LENGTH_Y, LENGTH_Z), jnp.float32) ** shard_levels(splits[2], (PLANES, LENGTH_Y, LENGTH_Z), ((1, 8), (2, 4)), -0.2, 0.2)), 1.0, 2.0)
    return {"density": density, "velocity": velocity, "pressure": pressure}


adiabatic = 1.4
courant = 0.15
margin_cells = 4

def wrap_pad(fluid_state):
    return jnp.concatenate([fluid_state[..., -margin_cells:], fluid_state, fluid_state[..., :margin_cells]], axis=-1)

def face_states(values, cfl_number):
    length = values.shape[-1]
    left_cells = values[..., 1:length - 2]
    right_cells = values[..., 2:length - 1]
    halfway = (7.0 * (left_cells + right_cells) - (values[..., 0:length - 3] + values[..., 3:length])) / 12.0
    halfway = jnp.clip(halfway, jnp.minimum(left_cells, right_cells), jnp.maximum(left_cells, right_cells))
    minus_edge = halfway[..., 0:length - 4]
    plus_edge = halfway[..., 1:length - 3]
    centre = values[..., 2:length - 2]
    number = cfl_number[..., 2:length - 2]
    difference = plus_edge - minus_edge
    curvature = 6.0 * (centre - 0.5 * (minus_edge + plus_edge))
    weight = 1.0 - number * (2.0 / 3.0)
    right_face = plus_edge - 0.5 * number * (difference - weight * curvature)
    left_face = minus_edge + 0.5 * number * (difference + weight * curvature)
    lower_bound = jnp.minimum(values[..., 2:length - 3], values[..., 3:length - 2])
    upper_bound = jnp.maximum(values[..., 2:length - 3], values[..., 3:length - 2])
    return (jnp.clip(right_face[..., :-1], lower_bound, upper_bound), jnp.clip(left_face[..., 1:], lower_bound, upper_bound))

def riemann(density_left, density_right, normal_left, normal_right, pressure_left, pressure_right):
    imped_left = jnp.sqrt(adiabatic * pressure_left * density_left)
    imped_right = jnp.sqrt(adiabatic * pressure_right * density_right)
    shock_factor = (adiabatic + 1.0) / (2.0 * adiabatic)
    wave_left = imped_left
    wave_right = imped_right
    star_pressure = (wave_right * pressure_left + wave_left * pressure_right - wave_left * wave_right * (normal_right - normal_left)) / (wave_left + wave_right)
    for newton_turn in range(2):
        wave_left = imped_left * jnp.sqrt(1.0 + shock_factor * (star_pressure / pressure_left - 1.0))
        wave_right = imped_right * jnp.sqrt(1.0 + shock_factor * (star_pressure / pressure_right - 1.0))
        star_pressure = (wave_right * pressure_left + wave_left * pressure_right - wave_left * wave_right * (normal_right - normal_left)) / (wave_left + wave_right)
    star_speed = (wave_left * normal_left + wave_right * normal_right - (pressure_right - pressure_left)) / (wave_left + wave_right)
    return (star_pressure, star_speed)

def sweep(fluid_state, normal):
    density = fluid_state[0]
    pressure = fluid_state[4]
    velocity = [fluid_state[1], fluid_state[2], fluid_state[3]]
    length = density.shape[-1]
    cfl_number = courant * jnp.sqrt(adiabatic * pressure / density)
    density_left, density_right = face_states(density, cfl_number)
    normal_left, normal_right = face_states(velocity[normal - 1], cfl_number)
    pressure_left, pressure_right = face_states(pressure, cfl_number)
    star_pressure, star_speed = riemann(density_left, density_right, normal_left, normal_right, pressure_left, pressure_right)
    cell_mass = density[..., 3:length - 3]
    energy = pressure / ((adiabatic - 1.0) * density) + 0.5 * (velocity[0] * velocity[0] + velocity[1] * velocity[1] + velocity[2] * velocity[2])
    momentum_kick = courant * (star_pressure[..., 1:] - star_pressure[..., :-1]) / cell_mass
    star_work = star_pressure * star_speed
    work_done = courant * (star_work[..., 1:] - star_work[..., :-1]) / cell_mass
    new_width = 1.0 + courant * (star_speed[..., 1:] - star_speed[..., :-1])
    lagrange_density = cell_mass / new_width
    specific = []
    for component in range(3):
        specific_value = velocity[component][..., 3:length - 3]
        if component + 1 == normal:
            specific_value = specific_value - momentum_kick
        specific.append(specific_value)
    specific.append(energy[..., 3:length - 3] - work_done)
    displacement = courant * star_speed[..., 1:-1]
    carried_left = jnp.maximum(displacement, 0.0) * lagrange_density[..., :-1]
    carried_right = jnp.minimum(displacement, 0.0) * lagrange_density[..., 1:]
    mass_flux = carried_left + carried_right
    new_mass = cell_mass[..., 1:-1] - mass_flux[..., 1:] + mass_flux[..., :-1]
    remapped = []
    for quantity in specific:
        amount_flux = carried_left * quantity[..., :-1] + carried_right * quantity[..., 1:]
        remapped.append((cell_mass[..., 1:-1] * quantity[..., 1:-1] - amount_flux[..., 1:] + amount_flux[..., :-1]) / new_mass)
    kinetic = 0.5 * (remapped[0] * remapped[0] + remapped[1] * remapped[1] + remapped[2] * remapped[2])
    new_pressure = (adiabatic - 1.0) * new_mass * (remapped[3] - kinetic)
    return jnp.stack([new_mass, remapped[0], remapped[1], remapped[2], new_pressure])

def reference(density, velocity, pressure):

    def one_plane(plane_index):
        fluid_state = jnp.concatenate([lax.dynamic_index_in_dim(density, plane_index, 0, keepdims=True), lax.dynamic_index_in_dim(velocity, plane_index, 1, keepdims=False), lax.dynamic_index_in_dim(pressure, plane_index, 0, keepdims=True)], axis=0)
        turned_plane = jnp.swapaxes(fluid_state, 1, 2)
        turned_plane = jnp.swapaxes(sweep(wrap_pad(turned_plane), 2), 1, 2)
        return sweep(wrap_pad(turned_plane), 3)
    planes_out = lax.map(one_plane, jnp.arange(PLANES, dtype=jnp.int32))
    return (planes_out[:, 0], jnp.moveaxis(planes_out[:, 1:4], 0, 1), planes_out[:, 4])
```

```python
import functools

import jax
import jax.numpy as jnp
from jax import lax
from jax.experimental import pallas as pl
from jax.experimental.pallas import tpu as pltpu
from jax.sharding import PartitionSpec as P

NU = 0.15
PER_R = 1.0 / 1.2
SIGMA = 1.68**0.5
GUESS = (7.0 / 6.0) ** 0.5
UNROLL = 8
LANES = 128
EDGE = 4


def recip(x):
    return pltpu.reciprocal(x, approx=True)


def clip(x, lo, hi):
    return jnp.maximum(lo, jnp.minimum(x, hi))


def riemann(left, right):
    r_l, u_l, p_l = left
    r_r, u_r, p_r = right
    dp = p_r - p_l
    du = u_r - u_l
    j_l = lax.rsqrt(p_l * r_l)
    j_r = lax.rsqrt(p_r * r_r)
    rise = (j_r * dp - GUESS * du) * recip(j_l + j_r)
    a_l = (7.0 / 6.0) * p_l
    a_r = (1.0 / 6.0) * p_r + p_l
    for _ in range(2):
        j_l = lax.rsqrt(r_l * (a_l + rise))
        j_r = lax.rsqrt(r_r * (a_r + rise))
        rise = (j_r * dp - du) * recip(j_l + j_r)
    return p_l + rise, u_l - rise * j_l


EMPTY = (None,) * 9


def step(carry, new, conserved, emit):
    a3, a2, a1, h, bounds, face, star, lag, flux = carry
    nxt = [a2, a1, new] + [None] * 6
    if a3 is None:
        return tuple(nxt)
    lo = [jnp.minimum(x, y) for x, y in zip(a2, a1)]
    hi = [jnp.maximum(x, y) for x, y in zip(a2, a1)]
    h_new = tuple(
        clip((x2 + x1) * (7.0 / 12.0) - (x3 + x0) * (1.0 / 12.0), l, u)
        for x3, x2, x1, x0, l, u in zip(a3, a2, a1, new, lo, hi)
    )
    nxt[3] = h_new
    nxt[4] = tuple(lo + hi)
    if h is None:
        return tuple(nxt)
    sg = a2[2] * lax.rsqrt(a2[2] * a2[0]) * SIGMA
    m = 1.0 - sg
    b = sg * m
    e = sg + (b + b)
    base = [e * x - b * (am + ap) for x, am, ap in zip(a2, h, h_new)]
    nxt[5] = tuple(clip(x + m * ap, l, u) for x, ap, l, u in zip(base, h_new, lo, hi))
    if face is None:
        return tuple(nxt)
    left = [clip(x + m * am, l, u) for x, am, l, u in zip(base, h, bounds[:3], bounds[3:])]
    p_star, u_star = riemann(face, left)
    p_hat = 1.2 * p_star
    work = (p_hat + p_hat) * u_star
    nxt[6] = (u_star, p_hat, work)
    if star is None:
        return tuple(nxt)
    mass, m_n, m_s, m_t, en = conserved()
    m_n = m_n - p_hat + star[1]
    en = en - work + star[2]
    width = 1.0 + (u_star - star[0])
    cell = (mass, m_n, m_s, m_t, en)
    nxt[7] = cell + (width,)
    if lag is None:
        return tuple(nxt)
    ahead = star[0] > 0.0
    swept = star[0] * recip(jnp.where(ahead, lag[5], width))
    g = tuple(swept * jnp.where(ahead, x, y) for x, y in zip(lag[:5], cell))
    nxt[8] = g
    if flux is None:
        return tuple(nxt)
    emit(*[x - y + z for x, y, z in zip(lag[:5], g, flux)])
    return tuple(nxt)


def conserved_of(r, u, v, w, p):
    m_u, m_v, m_w = r * u, r * v, r * w
    return r, m_u, m_v, m_w, 6.0 * p + (m_u * u + m_v * v + m_w * w)


def after_y_values(mass, m_y, m_x, m_z, en):
    r = recip(mass)
    pi = (en - (m_x * m_x + m_y * m_y + m_z * m_z) * r) * (1.0 / 6.0)
    return mass, m_z * r, pi, m_x, m_y, en


def y_kernel(axes, planes, ny, halves, d_in, v_in, p_in, t_out, yb, ek, hr, ab, ho, send, recv):
    nrow, ncol = axes
    row, col = lax.axis_index("row"), lax.axis_index("col")
    up, dn = lax.rem(row + nrow - 1, nrow), lax.rem(row + 1, nrow)
    lf, rt = lax.rem(col + ncol - 1, ncol), lax.rem(col + 1, ncol)

    def at(r, c):
        return {"row": r, "col": c}

    around = [(up, col), (dn, col), (row, lf), (row, rt), (up, lf), (up, rt), (dn, lf), (dn, rt)]
    barrier = pltpu.get_barrier_semaphore()
    for r, c in around:
        pl.semaphore_signal(
            barrier, inc=1, device_id=at(r, c), device_id_type=pl.DeviceIdType.MESH
        )

    rows = planes * ny
    lane = lax.broadcasted_iota(jnp.int32, (8, LANES), 1)
    scales = (1.2, NU, NU, NU, NU * NU)
    refs = (
        d_in,
        v_in.at[pl.ds(0, rows)],
        v_in.at[pl.ds(rows, rows)],
        v_in.at[pl.ds(2 * rows, rows)],
        p_in,
    )

    def pack(b, _):
        y0 = pl.multiple_of(b * 8, 8)
        for f in range(5):
            acc = jnp.ones((8, LANES), jnp.float32)
            for p in range(planes):
                src = pl.ds(pl.multiple_of(p * ny + y0, 8), 8)
                last = refs[f][src, pl.ds((halves - 1) * LANES, LANES)]
                fst = refs[f][src, pl.ds(0, LANES)]
                last = pltpu.roll(last, EDGE * p + EDGE, 1)
                fst = pltpu.roll(fst, 32 + EDGE * p, 1)
                acc = jnp.where(lane // EDGE == p, last, acc)
                acc = jnp.where(lane // EDGE == 8 + p, fst, acc)
            ek[f, pl.ds(y0, 8), :] = acc * scales[f]
        return 0

    def spread(y, _):
        for f in range(5):
            for h in range(halves):
                x = ab[f, h, pl.ds(y, planes, stride=ny), :]
                yb[f, h, y + EDGE] = x * scales[f]
        return 0

    def place(b, _):
        r0 = pl.ds(pl.multiple_of(b * 8, 8), 8)
        for f in range(5):
            for h in range(halves):
                ab[f, h, r0, :] = refs[f][r0, pl.ds(h * LANES, LANES)]
        return 0

    lax.fori_loop(0, rows // 8, place, 0, unroll=4)
    lax.fori_loop(0, ny, spread, 0, unroll=4)
    lax.fori_loop(0, ny // 8, pack, 0)

    pl.semaphore_wait(barrier, len(around))

    def rows_of(start, size):
        return yb.at[:, :, pl.ds(start, size)]

    sends = [
        (rows_of(EDGE, EDGE), rows_of(ny + EDGE, EDGE), (up, col)),
        (rows_of(ny, EDGE), rows_of(0, EDGE), (dn, col)),
        (ek, hr.at[0, :, pl.ds(8, ny)], (row, rt)),
        (ek, hr.at[1, :, pl.ds(8, ny)], (row, lf)),
        (ek.at[:, pl.ds(ny - 8, 8)], hr.at[0, :, pl.ds(0, 8)], (dn, rt)),
        (ek.at[:, pl.ds(ny - 8, 8)], hr.at[1, :, pl.ds(0, 8)], (dn, lf)),
        (ek.at[:, pl.ds(0, 8)], hr.at[0, :, pl.ds(ny + 8, 8)], (up, rt)),
        (ek.at[:, pl.ds(0, 8)], hr.at[1, :, pl.ds(ny + 8, 8)], (up, lf)),
    ]
    copies = []
    for k, (src, dst, who) in enumerate(sends):
        copy = pltpu.make_async_remote_copy(
            src_ref=src,
            dst_ref=dst,
            send_sem=send.at[k],
            recv_sem=recv.at[k],
            device_id=at(*who),
            device_id_type=pl.DeviceIdType.MESH,
        )
        copy.start()
        copies.append(copy)

    def y_step(carry, c, h):
        def load(f, i):
            return yb[f, h, i + EDGE]

        def cons():
            r, x, y, z, p = (load(f, c - 3) for f in range(5))
            return conserved_of(r, y, x, z, p)

        def emit(*values):
            for f, x in enumerate(after_y_values(*values)):
                ab[f, h, pl.ds(c - EDGE, planes, stride=ny), :] = x

        return step(carry, tuple(load(f, c) for f in (0, 2, 4)), cons, emit)

    def y_steps(carries, start, count):
        for k in range(count):
            carries = tuple(y_step(carries[h], start + k, h) for h in range(halves))
        return carries

    carries = y_steps((EMPTY,) * halves, 0, 8)
    carries = lax.fori_loop(
        0,
        (ny - 8) // UNROLL,
        lambda i, cr: y_steps(cr, 8 + i * UNROLL, UNROLL),
        carries,
    )
    for copy in copies:
        copy.wait()
    y_steps(carries, ny, EDGE)
    y_steps((EMPTY,) * halves, -EDGE, 12)

    def z_load(f, c):
        s = pl.ds(8 + c, 8, stride=ny // 8)
        return jnp.where(lane < 32, hr[0, f, s, :], hr[1, f, s, :])

    carry = EMPTY
    for c in range(-EDGE, ny // 8 + EDGE):

        def cons(c=c):
            r, x, y, z, p = (z_load(f, c - 3) for f in range(5))
            return conserved_of(r, y, x, z, p)

        def emit(*values, c=c):
            for f, x in enumerate(after_y_values(*values)):
                ho[f, pl.ds(c - EDGE, 8, stride=ny // 8), :] = x

        carry = step(carry, tuple(z_load(f, c) for f in (0, 2, 4)), cons, emit)

    pitch = LANES + 16
    groups = rows // LANES
    for f in range(6):
        for g in range(groups):
            tiles = [ab[f, h, pl.ds(g * LANES, LANES), :].T for h in range(halves)]
            for h in range(halves):
                k = (g * halves + h) * pitch
                t_out[f, pl.ds(k + 8, LANES), :] = tiles[h]
                if h > 0:
                    t_out[f, pl.ds(k + EDGE, EDGE), :] = tiles[h - 1][LANES - EDGE :]
                if h + 1 < halves:
                    t_out[f, pl.ds(k + 8 + LANES, EDGE), :] = tiles[h + 1][:EDGE]
        edge = ho[f]
        both = jnp.concatenate([edge, pltpu.roll(edge, LANES - EDGE, 1)], axis=0).T
        for g in range(groups):
            k = g * halves * pitch
            t_out[f, pl.ds(k + EDGE, EDGE), :] = both[8 * g : 8 * g + EDGE]
            k = (g * halves + halves - 1) * pitch
            t_out[f, pl.ds(k + 8 + LANES, EDGE), :] = both[32 + 8 * g : 32 + 8 * g + EDGE]


def z_kernel(planes, ny, halves, t_in, d_out, v_out, p_out, zb):
    rows = planes * ny
    groups = rows // LANES
    pitch = LANES + 16
    out_pitch = LANES + 8
    blocks = groups * halves

    def load(f, c):
        return t_in[f, pl.ds(c + 8, blocks, stride=pitch), :]

    def z_step(carry, c):
        def cons():
            r, u, _, m_x, m_y, en = (load(f, c - 3) for f in range(6))
            return r, r * u, m_x, m_y, en

        def emit(mass, m_z, m_x, m_y, en):
            r = recip(mass)
            p = (en - (m_x * m_x + m_y * m_y + m_z * m_z) * r) * (1.0 / (6.0 * NU * NU))
            r = r * (1.0 / NU)
            for f, x in enumerate((mass * PER_R, m_x * r, m_y * r, m_z * r, p)):
                zb[f, pl.ds(c - EDGE, blocks, stride=out_pitch), :] = x

        return step(carry, tuple(load(f, c) for f in range(3)), cons, emit)

    carry = EMPTY
    for c in range(-EDGE, EDGE):
        carry = z_step(carry, c)

    def turn(i, carry):
        for k in range(UNROLL):
            carry = z_step(carry, EDGE + i * UNROLL + k)
        return carry

    lax.fori_loop(0, LANES // UNROLL, turn, carry)

    outs = [
        d_out,
        v_out.at[pl.ds(0, rows)],
        v_out.at[pl.ds(rows, rows)],
        v_out.at[pl.ds(2 * rows, rows)],
        p_out,
    ]
    for f in range(5):
        for g in range(groups):
            for h in range(halves):
                k = (g * halves + h) * out_pitch
                outs[f][pl.ds(g * LANES, LANES), pl.ds(h * LANES, LANES)] = zb[
                    f, pl.ds(k, LANES), :
                ].T


def on_device(axes, density, velocity, pressure):
    planes, ny, nz = density.shape
    rows, halves = planes * ny, nz // LANES
    pitch = LANES + 16
    blocks = rows // LANES * halves
    f32 = jnp.float32
    vmem = pl.BlockSpec(memory_space=pltpu.VMEM)
    turned = pl.pallas_call(
        functools.partial(y_kernel, axes, planes, ny, halves),
        out_shape=jax.ShapeDtypeStruct((6, blocks * pitch, LANES), f32),
        in_specs=[vmem] * 3,
        out_specs=vmem,
        scratch_shapes=[
            pltpu.VMEM((5, halves, ny + 2 * EDGE, planes, LANES), f32),
            pltpu.VMEM((5, ny, LANES), f32),
            pltpu.VMEM((2, 5, ny + 16, LANES), f32),
            pltpu.VMEM((6, halves, rows, LANES), f32),
            pltpu.VMEM((6, ny, LANES), f32),
            pltpu.SemaphoreType.DMA((8,)),
            pltpu.SemaphoreType.DMA((8,)),
        ],
        compiler_params=pltpu.CompilerParams(
            collective_id=0, has_side_effects=True, vmem_limit_bytes=40 * 2**20
        ),
    )(density.reshape(rows, nz), velocity.reshape(3 * rows, nz), pressure.reshape(rows, nz))
    d, v, p = pl.pallas_call(
        functools.partial(z_kernel, planes, ny, halves),
        out_shape=[
            jax.ShapeDtypeStruct((rows, nz), f32),
            jax.ShapeDtypeStruct((3 * rows, nz), f32),
            jax.ShapeDtypeStruct((rows, nz), f32),
        ],
        in_specs=[vmem],
        out_specs=[vmem] * 3,
        scratch_shapes=[pltpu.VMEM((5, blocks * (LANES + 8), LANES), f32)],
        compiler_params=pltpu.CompilerParams(vmem_limit_bytes=40 * 2**20),
    )(turned)
    return d.reshape(density.shape), v.reshape(velocity.shape), p.reshape(density.shape)


def solution(mesh):
    field = P(None, "row", "col")
    vector = P(None, None, "row", "col")
    axes = (mesh.shape["row"], mesh.shape["col"])
    return jax.shard_map(
        functools.partial(on_device, axes),
        mesh=mesh,
        in_specs=(field, vector, field),
        out_specs=(field, vector, field),
        check_vma=False,
    )
```

```python
import functools

import jax
import jax.numpy as jnp
from jax import lax
from jax.experimental import pallas as pl
from jax.experimental.pallas import tpu as pltpu
from jax.sharding import PartitionSpec as P

NU = 0.15
PER_R = 1.0 / 1.2
SIGMA = 1.68**0.5
GUESS = (7.0 / 6.0) ** 0.5
UNROLL = 8
LANES = 128
EDGE = 4


def recip(x):
    return pltpu.reciprocal(x, approx=True)


def clip(x, lo, hi):
    return jnp.maximum(lo, jnp.minimum(x, hi))


def riemann(left, right):
    r_l, u_l, p_l = left
    r_r, u_r, p_r = right
    dp = p_r - p_l
    du = u_r - u_l
    j_l = lax.rsqrt(p_l * r_l)
    j_r = lax.rsqrt(p_r * r_r)
    rise = (j_r * dp - GUESS * du) * recip(j_l + j_r)
    a_l = (7.0 / 6.0) * p_l
    a_r = (1.0 / 6.0) * p_r + p_l
    for _ in range(2):
        j_l = lax.rsqrt(r_l * (a_l + rise))
        j_r = lax.rsqrt(r_r * (a_r + rise))
        rise = (j_r * dp - du) * recip(j_l + j_r)
    return p_l + rise, u_l - rise * j_l


EMPTY = (None,) * 9


def step(carry, new, conserved, emit):
    a3, a2, a1, h, bounds, face, star, lag, flux = carry
    nxt = [a2, a1, new] + [None] * 6
    if a3 is None:
        return tuple(nxt)
    lo = [jnp.minimum(x, y) for x, y in zip(a2, a1)]
    hi = [jnp.maximum(x, y) for x, y in zip(a2, a1)]
    h_new = tuple(
        clip((x2 + x1) * (7.0 / 12.0) - (x3 + x0) * (1.0 / 12.0), l, u)
        for x3, x2, x1, x0, l, u in zip(a3, a2, a1, new, lo, hi)
    )
    nxt[3] = h_new
    nxt[4] = tuple(lo + hi)
    if h is None:
        return tuple(nxt)
    sg = a2[2] * lax.rsqrt(a2[2] * a2[0]) * SIGMA
    m = 1.0 - sg
    b = sg * m
    e = sg + (b + b)
    base = [e * x - b * (am + ap) for x, am, ap in zip(a2, h, h_new)]
    nxt[5] = tuple(clip(x + m * ap, l, u) for x, ap, l, u in zip(base, h_new, lo, hi))
    if face is None:
        return tuple(nxt)
    left = [clip(x + m * am, l, u) for x, am, l, u in zip(base, h, bounds[:3], bounds[3:])]
    p_star, u_star = riemann(face, left)
    p_hat = 1.2 * p_star
    work = (p_hat + p_hat) * u_star
    nxt[6] = (u_star, p_hat, work)
    if star is None:
        return tuple(nxt)
    mass, m_n, m_s, m_t, en = conserved()
    m_n = m_n - p_hat + star[1]
    en = en - work + star[2]
    width = 1.0 + (u_star - star[0])
    cell = (mass, m_n, m_s, m_t, en)
    nxt[7] = cell + (width,)
    if lag is None:
        return tuple(nxt)
    ahead = star[0] > 0.0
    swept = star[0] * recip(jnp.where(ahead, lag[5], width))
    g = tuple(swept * jnp.where(ahead, x, y) for x, y in zip(lag[:5], cell))
    nxt[8] = g
    if flux is None:
        return tuple(nxt)
    emit(*[x - y + z for x, y, z in zip(lag[:5], g, flux)])
    return tuple(nxt)


def conserved_of(r, u, v, w, p):
    m_u, m_v, m_w = r * u, r * v, r * w
    return r, m_u, m_v, m_w, 6.0 * p + (m_u * u + m_v * v + m_w * w)


def after_y_values(mass, m_y, m_x, m_z, en):
    r = recip(mass)
    pi = (en - (m_x * m_x + m_y * m_y + m_z * m_z) * r) * (1.0 / 6.0)
    return mass, m_z * r, pi, m_x, m_y, en


def y_kernel(
    axes, planes, ny, halves, d_in, v_in, p_in, t_out,
    xin, yb, ek, pk, pr, cr, hr, ab, ho, load_sem, send, recv,
):
    nrow, ncol = axes
    row, col = lax.axis_index("row"), lax.axis_index("col")
    up, dn = lax.rem(row + nrow - 1, nrow), lax.rem(row + 1, nrow)
    lf, rt = lax.rem(col + ncol - 1, ncol), lax.rem(col + 1, ncol)

    def at(r, c):
        return {"row": r, "col": c}

    around = [(up, col), (dn, col), (row, lf), (row, rt), (up, lf), (up, rt), (dn, lf), (dn, rt)]
    barrier = pltpu.get_barrier_semaphore()
    for r, c in around:
        pl.semaphore_signal(
            barrier, inc=1, device_id=at(r, c), device_id_type=pl.DeviceIdType.MESH
        )

    rows = planes * ny
    lane = lax.broadcasted_iota(jnp.int32, (8, LANES), 1)
    scales = (1.2, NU, NU, NU, NU * NU)
    refs = (
        d_in,
        v_in.at[pl.ds(0, rows)],
        v_in.at[pl.ds(rows, rows)],
        v_in.at[pl.ds(2 * rows, rows)],
        p_in,
    )
    loads = []
    for f in range(5):
        for h in range(halves):
            copy = pltpu.make_async_copy(
                refs[f].at[:, pl.ds(h * LANES, LANES)], xin.at[f, h], load_sem.at[f, h]
            )
            copy.start()
            loads.append(copy)

    def spread(y, _):
        for f in range(5):
            for h in range(halves):
                x = xin[f, h, pl.ds(y, planes, stride=ny), :]
                yb[f, h, y + EDGE] = x * scales[f]
        return 0

    def pack(b, _):
        y0 = pl.multiple_of(b * 8, 8)
        for f in range(5):
            acc = jnp.ones((8, LANES), jnp.float32)
            for p in range(planes):
                src = pl.ds(pl.multiple_of(p * ny + y0, 8), 8)
                last = pltpu.roll(xin[f, halves - 1, src, :], EDGE * p + EDGE, 1)
                fst = pltpu.roll(xin[f, 0, src, :], 32 + EDGE * p, 1)
                acc = jnp.where(lane // EDGE == p, last, acc)
                acc = jnp.where(lane // EDGE == 8 + p, fst, acc)
            ek[f, pl.ds(y0, 8), :] = acc * scales[f]
        return 0

    copies = []

    def remote(k, src, dst, who):
        copy = pltpu.make_async_remote_copy(
            src_ref=src,
            dst_ref=dst,
            send_sem=send.at[k],
            recv_sem=recv.at[k],
            device_id=at(*who),
            device_id_type=pl.DeviceIdType.MESH,
        )
        copy.start()
        copies.append(copy)

    def rows_of(start, size):
        return yb.at[:, :, pl.ds(start, size)]

    for copy in loads:
        copy.wait()
    for y in (*range(EDGE), *range(ny - EDGE, ny)):
        spread(y, 0)
    pl.semaphore_wait(barrier, len(around))
    remote(0, rows_of(EDGE, EDGE), rows_of(ny + EDGE, EDGE), (up, col))
    remote(1, rows_of(ny, EDGE), rows_of(0, EDGE), (dn, col))

    lax.fori_loop(0, ny // 8, pack, 0)
    fold = LANES // 32
    part = ny // fold
    for f in range(5):
        for b in range(part // 8):
            for side in range(2):
                acc = None
                for q in range(fold):
                    x = ek[f, pl.ds(q * part + b * 8, 8), :]
                    turn = (32 * (q - side)) % LANES
                    x = pltpu.roll(x, turn, 1) if turn else x
                    acc = x if acc is None else jnp.where(lane // 32 == q, x, acc)
                pk[side, f, pl.ds(b * 8, 8), :] = acc
    remote(2, pk.at[0], pr.at[0], (row, rt))
    remote(3, pk.at[1], pr.at[1], (row, lf))
    remote(4, ek.at[:, pl.ds(ny - 8, 8)], cr.at[0, 0], (dn, rt))
    remote(5, ek.at[:, pl.ds(ny - 8, 8)], cr.at[1, 0], (dn, lf))
    remote(6, ek.at[:, pl.ds(0, 8)], cr.at[0, 1], (up, rt))
    remote(7, ek.at[:, pl.ds(0, 8)], cr.at[1, 1], (up, lf))
    lax.fori_loop(EDGE, ny - EDGE, spread, 0, unroll=4)

    def y_step(carry, c, h):
        def load(f, i):
            return yb[f, h, i + EDGE]

        def cons():
            r, x, y, z, p = (load(f, c - 3) for f in range(5))
            return conserved_of(r, y, x, z, p)

        def emit(*values):
            for f, x in enumerate(after_y_values(*values)):
                ab[f, h, pl.ds(c - EDGE, planes, stride=ny), :] = x

        return step(carry, tuple(load(f, c) for f in (0, 2, 4)), cons, emit)

    def y_steps(carries, start, count):
        for k in range(count):
            carries = tuple(y_step(carries[h], start + k, h) for h in range(halves))
        return carries

    carries = y_steps((EMPTY,) * halves, 0, 8)
    carries = lax.fori_loop(
        0,
        (ny - 8) // UNROLL,
        lambda i, cr: y_steps(cr, 8 + i * UNROLL, UNROLL),
        carries,
    )
    for copy in copies[:2]:
        copy.wait()
    y_steps(carries, ny, EDGE)
    y_steps((EMPTY,) * halves, -EDGE, 12)

    for copy in copies[2:]:
        copy.wait()
    for f in range(5):
        for end, start in ((0, 0), (1, ny + 8)):
            hr[f, pl.ds(start, 8), :] = jnp.where(lane < 32, cr[0, end, f], cr[1, end, f])
        for b in range(part // 8):
            for q in range(fold):
                x = [pr[side, f, pl.ds(b * 8, 8), :] for side in range(2)]
                for side in range(2):
                    turn = (32 * (side - q)) % LANES
                    x[side] = pltpu.roll(x[side], turn, 1) if turn else x[side]
                hr[f, pl.ds(8 + q * part + b * 8, 8), :] = jnp.where(lane < 32, *x)

    def z_load(f, c):
        return hr[f, pl.ds(8 + c, 8, stride=ny // 8), :]

    carry = EMPTY
    for c in range(-EDGE, ny // 8 + EDGE):

        def cons(c=c):
            r, x, y, z, p = (z_load(f, c - 3) for f in range(5))
            return conserved_of(r, y, x, z, p)

        def emit(*values, c=c):
            for f, x in enumerate(after_y_values(*values)):
                ho[f, pl.ds(c - EDGE, 8, stride=ny // 8), :] = x

        carry = step(carry, tuple(z_load(f, c) for f in (0, 2, 4)), cons, emit)

    pitch = LANES + 16
    groups = rows // LANES
    for f in range(6):
        for g in range(groups):
            tiles = [ab[f, h, pl.ds(g * LANES, LANES), :].T for h in range(halves)]
            for h in range(halves):
                k = (g * halves + h) * pitch
                t_out[f, pl.ds(k + 8, LANES), :] = tiles[h]
                if h > 0:
                    t_out[f, pl.ds(k + EDGE, EDGE), :] = tiles[h - 1][LANES - EDGE :]
                if h + 1 < halves:
                    t_out[f, pl.ds(k + 8 + LANES, EDGE), :] = tiles[h + 1][:EDGE]
        edge = ho[f]
        both = jnp.concatenate([edge, pltpu.roll(edge, LANES - EDGE, 1)], axis=0).T
        for g in range(groups):
            k = g * halves * pitch
            t_out[f, pl.ds(k + EDGE, EDGE), :] = both[8 * g : 8 * g + EDGE]
            k = (g * halves + halves - 1) * pitch
            t_out[f, pl.ds(k + 8 + LANES, EDGE), :] = both[32 + 8 * g : 32 + 8 * g + EDGE]


def z_kernel(planes, ny, halves, t_in, d_out, v_out, p_out, zb):
    rows = planes * ny
    groups = rows // LANES
    pitch = LANES + 16
    out_pitch = LANES + 8
    blocks = groups * halves

    def load(f, c):
        return t_in[f, pl.ds(c + 8, blocks, stride=pitch), :]

    def z_step(carry, c):
        def cons():
            r, u, _, m_x, m_y, en = (load(f, c - 3) for f in range(6))
            return r, r * u, m_x, m_y, en

        def emit(mass, m_z, m_x, m_y, en):
            r = recip(mass)
            p = (en - (m_x * m_x + m_y * m_y + m_z * m_z) * r) * (1.0 / (6.0 * NU * NU))
            r = r * (1.0 / NU)
            for f, x in enumerate((mass * PER_R, m_x * r, m_y * r, m_z * r, p)):
                zb[f, pl.ds(c - EDGE, blocks, stride=out_pitch), :] = x

        return step(carry, tuple(load(f, c) for f in range(3)), cons, emit)

    carry = EMPTY
    for c in range(-EDGE, EDGE):
        carry = z_step(carry, c)

    def turn(i, carry):
        for k in range(UNROLL):
            carry = z_step(carry, EDGE + i * UNROLL + k)
        return carry

    lax.fori_loop(0, LANES // UNROLL, turn, carry)

    outs = [
        d_out,
        v_out.at[pl.ds(0, rows)],
        v_out.at[pl.ds(rows, rows)],
        v_out.at[pl.ds(2 * rows, rows)],
        p_out,
    ]
    for f in range(5):
        for g in range(groups):
            for h in range(halves):
                k = (g * halves + h) * out_pitch
                outs[f][pl.ds(g * LANES, LANES), pl.ds(h * LANES, LANES)] = zb[
                    f, pl.ds(k, LANES), :
                ].T


def on_device(axes, density, velocity, pressure):
    planes, ny, nz = density.shape
    rows, halves = planes * ny, nz // LANES
    pitch = LANES + 16
    blocks = rows // LANES * halves
    f32 = jnp.float32
    vmem = pl.BlockSpec(memory_space=pltpu.VMEM)
    turned = pl.pallas_call(
        functools.partial(y_kernel, axes, planes, ny, halves),
        out_shape=jax.ShapeDtypeStruct((6, blocks * pitch, LANES), f32),
        in_specs=[pl.BlockSpec(memory_space=pltpu.HBM)] * 3,
        out_specs=vmem,
        scratch_shapes=[
            pltpu.VMEM((5, halves, rows, LANES), f32),
            pltpu.VMEM((5, halves, ny + 2 * EDGE, planes, LANES), f32),
            pltpu.VMEM((5, ny, LANES), f32),
            pltpu.VMEM((2, 5, ny // (LANES // 32), LANES), f32),
            pltpu.VMEM((2, 5, ny // (LANES // 32), LANES), f32),
            pltpu.VMEM((2, 2, 5, 8, LANES), f32),
            pltpu.VMEM((5, ny + 16, LANES), f32),
            pltpu.VMEM((6, halves, rows, LANES), f32),
            pltpu.VMEM((6, ny, LANES), f32),
            pltpu.SemaphoreType.DMA((5, halves)),
            pltpu.SemaphoreType.DMA((8,)),
            pltpu.SemaphoreType.DMA((8,)),
        ],
        compiler_params=pltpu.CompilerParams(
            collective_id=0, has_side_effects=True, vmem_limit_bytes=40 * 2**20
        ),
    )(
        *[
            pltpu.with_memory_space_constraint(x.reshape(-1, nz), pltpu.HBM)
            for x in (density, velocity, pressure)
        ]
    )
    d, v, p = pl.pallas_call(
        functools.partial(z_kernel, planes, ny, halves),
        out_shape=[
            jax.ShapeDtypeStruct((rows, nz), f32),
            jax.ShapeDtypeStruct((3 * rows, nz), f32),
            jax.ShapeDtypeStruct((rows, nz), f32),
        ],
        in_specs=[vmem],
        out_specs=[vmem] * 3,
        scratch_shapes=[pltpu.VMEM((5, blocks * (LANES + 8), LANES), f32)],
        compiler_params=pltpu.CompilerParams(vmem_limit_bytes=40 * 2**20),
    )(turned)
    return d.reshape(density.shape), v.reshape(velocity.shape), p.reshape(density.shape)


def solution(mesh):
    field = P(None, "row", "col")
    vector = P(None, None, "row", "col")
    axes = (mesh.shape["row"], mesh.shape["col"])
    return jax.shard_map(
        functools.partial(on_device, axes),
        mesh=mesh,
        in_specs=(field, vector, field),
        out_specs=(field, vector, field),
        check_vma=False,
    )
```

```python
import functools

import jax
import jax.numpy as jnp
from jax import lax
from jax.experimental import pallas as pl
from jax.experimental.pallas import tpu as pltpu
from jax.sharding import PartitionSpec as P

NU = 0.15
PER_R = 1.0 / 1.2
SIGMA = 1.68**0.5
GUESS = (7.0 / 6.0) ** 0.5
UNROLL = 8
UNROLL_Z = 32
LANES = 128
EDGE = 4


def recip(x):
    return pltpu.reciprocal(x, approx=True)


def clip(x, lo, hi):
    return jnp.maximum(lo, jnp.minimum(x, hi))


def riemann(left, right):
    r_l, u_l, p_l = left
    r_r, u_r, p_r = right
    dp = p_r - p_l
    du = u_r - u_l
    j_l = lax.rsqrt(p_l * r_l)
    j_r = lax.rsqrt(p_r * r_r)
    rise = (j_r * dp - GUESS * du) * recip(j_l + j_r)
    a_l = (7.0 / 6.0) * p_l
    a_r = (1.0 / 6.0) * p_r + p_l
    for _ in range(2):
        j_l = lax.rsqrt(r_l * (a_l + rise))
        j_r = lax.rsqrt(r_r * (a_r + rise))
        rise = (j_r * dp - du) * recip(j_l + j_r)
    return p_l + rise, u_l - rise * j_l


EMPTY = (None,) * 9


def step(carry, new, conserved, emit):
    a3, a2, a1, h, bounds, face, star, lag, flux = carry
    nxt = [a2, a1, new] + [None] * 6
    if a3 is None:
        return tuple(nxt)
    lo = [jnp.minimum(x, y) for x, y in zip(a2, a1)]
    hi = [jnp.maximum(x, y) for x, y in zip(a2, a1)]
    h_new = tuple(
        clip((x2 + x1) * (7.0 / 12.0) - (x3 + x0) * (1.0 / 12.0), l, u)
        for x3, x2, x1, x0, l, u in zip(a3, a2, a1, new, lo, hi)
    )
    nxt[3] = h_new
    nxt[4] = tuple(lo + hi)
    if h is None:
        return tuple(nxt)
    sg = a2[2] * lax.rsqrt(a2[2] * a2[0]) * SIGMA
    m = 1.0 - sg
    b = sg * m
    e = sg + (b + b)
    base = [e * x - b * (am + ap) for x, am, ap in zip(a2, h, h_new)]
    nxt[5] = tuple(clip(x + m * ap, l, u) for x, ap, l, u in zip(base, h_new, lo, hi))
    if face is None:
        return tuple(nxt)
    left = [clip(x + m * am, l, u) for x, am, l, u in zip(base, h, bounds[:3], bounds[3:])]
    p_star, u_star = riemann(face, left)
    p_hat = 1.2 * p_star
    work = (p_hat + p_hat) * u_star
    nxt[6] = (u_star, p_hat, work)
    if star is None:
        return tuple(nxt)
    mass, m_n, m_s, m_t, en = conserved()
    m_n = m_n - p_hat + star[1]
    en = en - work + star[2]
    width = 1.0 + (u_star - star[0])
    cell = (mass, m_n, m_s, m_t, en)
    nxt[7] = cell + (width,)
    if lag is None:
        return tuple(nxt)
    ahead = star[0] > 0.0
    swept = star[0] * recip(jnp.where(ahead, lag[5], width))
    g = tuple(swept * jnp.where(ahead, x, y) for x, y in zip(lag[:5], cell))
    nxt[8] = g
    if flux is None:
        return tuple(nxt)
    emit(*[x - y + z for x, y, z in zip(lag[:5], g, flux)])
    return tuple(nxt)


def conserved_of(r, u, v, w, p):
    m_u, m_v, m_w = r * u, r * v, r * w
    return r, m_u, m_v, m_w, 6.0 * p + (m_u * u + m_v * v + m_w * w)


def after_y_values(mass, m_y, m_x, m_z, en):
    r = recip(mass)
    pi = (en - (m_x * m_x + m_y * m_y + m_z * m_z) * r) * (1.0 / 6.0)
    return mass, m_z * r, pi, m_x, m_y, en


def y_kernel(
    axes, planes, ny, halves, d_in, v_in, p_in, t_out,
    xin, yb, ek, pk, pr, cr, hr, ab, ho, load_sem, send, recv,
):
    nrow, ncol = axes
    row, col = lax.axis_index("row"), lax.axis_index("col")
    up, dn = lax.rem(row + nrow - 1, nrow), lax.rem(row + 1, nrow)
    lf, rt = lax.rem(col + ncol - 1, ncol), lax.rem(col + 1, ncol)

    def at(r, c):
        return {"row": r, "col": c}

    around = [(up, col), (dn, col), (row, lf), (row, rt), (up, lf), (up, rt), (dn, lf), (dn, rt)]
    barrier = pltpu.get_barrier_semaphore()
    for r, c in around:
        pl.semaphore_signal(
            barrier, inc=1, device_id=at(r, c), device_id_type=pl.DeviceIdType.MESH
        )

    rows = planes * ny
    lane = lax.broadcasted_iota(jnp.int32, (8, LANES), 1)
    scales = (1.2, NU, NU * NU, NU, NU)
    refs = (
        d_in,
        v_in.at[pl.ds(rows, rows)],
        p_in,
        v_in.at[pl.ds(0, rows)],
        v_in.at[pl.ds(2 * rows, rows)],
    )
    loads = []
    for f in range(5):
        for h in range(halves):
            copy = pltpu.make_async_copy(
                refs[f].at[:, pl.ds(h * LANES, LANES)], xin.at[f, h], load_sem.at[f, h]
            )
            copy.start()
            loads.append(copy)

    def spread(y, _):
        for f in range(5):
            for h in range(halves):
                x = xin[f, h, pl.ds(y, planes, stride=ny), :]
                yb[f, h, y + EDGE] = x * scales[f]
        return 0

    def pack(b, _):
        y0 = pl.multiple_of(b * 8, 8)
        for f in range(5):
            acc = jnp.ones((8, LANES), jnp.float32)
            for p in range(planes):
                src = pl.ds(pl.multiple_of(p * ny + y0, 8), 8)
                x = jnp.where(lane < EDGE, xin[f, 0, src, :], xin[f, halves - 1, src, :])
                x = pltpu.roll(x, 2 * EDGE * p + EDGE, 1)
                acc = jnp.where(lane // (2 * EDGE) == p, x, acc)
            ek[f, pl.ds(y0, 8), :] = acc * scales[f]
        return 0

    copies = []

    def remote(k, src, dst, who):
        copy = pltpu.make_async_remote_copy(
            src_ref=src,
            dst_ref=dst,
            send_sem=send.at[k],
            recv_sem=recv.at[k],
            device_id=at(*who),
            device_id_type=pl.DeviceIdType.MESH,
        )
        copy.start()
        copies.append(copy)

    def rows_of(start):
        return yb.at[pl.ds(0, 3), :, pl.ds(start, EDGE)]

    def row_of(y):
        return yb.at[pl.ds(3, 2), :, pl.ds(y, 1)]

    for copy in loads:
        copy.wait()
    for y in (*range(EDGE), *range(ny - EDGE, ny)):
        spread(y, 0)
    lax.fori_loop(0, ny // 8, pack, 0, unroll=2)
    fold = LANES // 32
    slot = lane // 64 * 2 + lane // EDGE % 2
    part = ny // fold
    for f in range(5):
        for b in range(part // 8):
            for side in range(2):
                acc = None
                for q in range(fold):
                    x = ek[f, pl.ds(q * part + b * 8, 8), :]
                    turn = (64 * (q // 2) + EDGE * (q % 2 - side)) % LANES
                    x = pltpu.roll(x, turn, 1) if turn else x
                    acc = x if acc is None else jnp.where(slot == q, x, acc)
                pk[side, f, pl.ds(b * 8, 8), :] = acc
    pl.semaphore_wait(barrier, len(around))
    remote(0, rows_of(EDGE), rows_of(ny + EDGE), (up, col))
    remote(1, rows_of(ny), rows_of(0), (dn, col))
    remote(8, row_of(EDGE), row_of(ny + EDGE), (up, col))
    remote(9, row_of(ny + EDGE - 1), row_of(EDGE - 1), (dn, col))
    remote(2, pk.at[0], pr.at[0], (row, rt))
    remote(3, pk.at[1], pr.at[1], (row, lf))
    remote(4, ek.at[:, pl.ds(ny - 8, 8)], cr.at[0, 0], (dn, rt))
    remote(5, ek.at[:, pl.ds(ny - 8, 8)], cr.at[1, 0], (dn, lf))
    remote(6, ek.at[:, pl.ds(0, 8)], cr.at[0, 1], (up, rt))
    remote(7, ek.at[:, pl.ds(0, 8)], cr.at[1, 1], (up, lf))
    lax.fori_loop(EDGE, ny - EDGE, spread, 0, unroll=4)

    def y_step(carry, c, h):
        def load(f, i):
            return yb[f, h, i + EDGE]

        def cons():
            r, y, p, x, z = (load(f, c - 3) for f in range(5))
            return conserved_of(r, y, x, z, p)

        def emit(*values):
            for f, x in enumerate(after_y_values(*values)):
                ab[f, h, pl.ds(c - EDGE, planes, stride=ny), :] = x

        return step(carry, tuple(load(f, c) for f in range(3)), cons, emit)

    def y_steps(carries, start, count):
        for k in range(count):
            carries = tuple(y_step(carries[h], start + k, h) for h in range(halves))
        return carries

    carries = y_steps((EMPTY,) * halves, 0, 8)
    carries = lax.fori_loop(
        0,
        (ny - 8) // UNROLL,
        lambda i, cr: y_steps(cr, 8 + i * UNROLL, UNROLL),
        carries,
    )
    for copy in copies:
        copy.wait()

    for f in range(5):
        for end, start in ((0, 0), (1, ny + 8)):
            hr[f, pl.ds(start, 8), :] = jnp.where(slot % 2 == 0, cr[0, end, f], cr[1, end, f])
        for b in range(part // 8):
            for q in range(fold):
                x = [pr[side, f, pl.ds(b * 8, 8), :] for side in range(2)]
                for side in range(2):
                    turn = (-64 * (q // 2) + EDGE * (side - q % 2)) % LANES
                    x[side] = pltpu.roll(x[side], turn, 1) if turn else x[side]
                hr[f, pl.ds(8 + q * part + b * 8, 8), :] = jnp.where(slot % 2 == 0, *x)

    def z_load(f, c):
        return hr[f, pl.ds(8 + c, 8, stride=ny // 8), :]

    def z_edge(carry, c):
        def cons():
            r, y, p, x, z = (z_load(f, c - 3) for f in range(5))
            return conserved_of(r, y, x, z, p)

        def emit(*values):
            for f, x in enumerate(after_y_values(*values)):
                ho[f, pl.ds(c - EDGE, 8, stride=ny // 8), :] = x

        return step(carry, tuple(z_load(f, c) for f in range(3)), cons, emit)

    carry, first = EMPTY, (EMPTY,) * halves
    for k in range(ny // 8 + 2 * EDGE):
        carry = z_edge(carry, k - EDGE)
        if k < 3 * EDGE:
            first = y_steps(first, k - EDGE, 1)
        if k < EDGE:
            carries = y_steps(carries, ny + k, 1)

    pitch = LANES + 16
    groups = rows // LANES
    for f in range(6):
        for g in range(groups):
            tiles = [ab[f, h, pl.ds(g * LANES, LANES), :].T for h in range(halves)]
            for h in range(halves):
                k = (g * halves + h) * pitch
                t_out[f, pl.ds(k + 8, LANES), :] = tiles[h]
                if h > 0:
                    t_out[f, pl.ds(k + EDGE, EDGE), :] = tiles[h - 1][LANES - EDGE :]
                if h + 1 < halves:
                    t_out[f, pl.ds(k + 8 + LANES, EDGE), :] = tiles[h + 1][:EDGE]
        edge = ho[f]
        both = jnp.concatenate([edge, pltpu.roll(edge, LANES - 2 * EDGE, 1)], axis=0).T
        for g in range(groups):
            k = g * halves * pitch
            t_out[f, pl.ds(k + EDGE, EDGE), :] = both[16 * g : 16 * g + EDGE]
            k = (g * halves + halves - 1) * pitch
            t_out[f, pl.ds(k + 8 + LANES, EDGE), :] = both[16 * g + EDGE : 16 * g + 2 * EDGE]


def z_kernel(planes, ny, halves, t_in, d_out, v_out, p_out, zb):
    rows = planes * ny
    groups = rows // LANES
    pitch = LANES + 16
    out_pitch = LANES + 8
    blocks = groups * halves

    def load(f, c):
        return t_in[f, pl.ds(c + 8, blocks, stride=pitch), :]

    def z_step(carry, c):
        def cons():
            r, u, _, m_x, m_y, en = (load(f, c - 3) for f in range(6))
            return r, r * u, m_x, m_y, en

        def emit(mass, m_z, m_x, m_y, en):
            r = recip(mass)
            p = (en - (m_x * m_x + m_y * m_y + m_z * m_z) * r) * (1.0 / (6.0 * NU * NU))
            r = r * (1.0 / NU)
            for f, x in enumerate((mass * PER_R, m_x * r, m_y * r, m_z * r, p)):
                zb[f, pl.ds(c - EDGE, blocks, stride=out_pitch), :] = x

        return step(carry, tuple(load(f, c) for f in range(3)), cons, emit)

    carry = EMPTY
    for c in range(-EDGE, EDGE):
        carry = z_step(carry, c)

    def turn(i, carry):
        for k in range(UNROLL_Z):
            carry = z_step(carry, EDGE + i * UNROLL_Z + k)
        return carry

    lax.fori_loop(0, LANES // UNROLL_Z, turn, carry)

    outs = [
        d_out,
        v_out.at[pl.ds(0, rows)],
        v_out.at[pl.ds(rows, rows)],
        v_out.at[pl.ds(2 * rows, rows)],
        p_out,
    ]
    for f in range(5):
        for g in range(groups):
            for h in range(halves):
                k = (g * halves + h) * out_pitch
                outs[f][pl.ds(g * LANES, LANES), pl.ds(h * LANES, LANES)] = zb[
                    f, pl.ds(k, LANES), :
                ].T


def on_device(axes, density, velocity, pressure):
    planes, ny, nz = density.shape
    rows, halves = planes * ny, nz // LANES
    pitch = LANES + 16
    blocks = rows // LANES * halves
    f32 = jnp.float32
    vmem = pl.BlockSpec(memory_space=pltpu.VMEM)
    turned = pl.pallas_call(
        functools.partial(y_kernel, axes, planes, ny, halves),
        out_shape=jax.ShapeDtypeStruct((6, blocks * pitch, LANES), f32),
        in_specs=[pl.BlockSpec(memory_space=pltpu.HBM)] * 3,
        out_specs=vmem,
        scratch_shapes=[
            pltpu.VMEM((5, halves, rows, LANES), f32),
            pltpu.VMEM((5, halves, ny + 2 * EDGE, planes, LANES), f32),
            pltpu.VMEM((5, ny, LANES), f32),
            pltpu.VMEM((2, 5, ny // (LANES // 32), LANES), f32),
            pltpu.VMEM((2, 5, ny // (LANES // 32), LANES), f32),
            pltpu.VMEM((2, 2, 5, 8, LANES), f32),
            pltpu.VMEM((5, ny + 16, LANES), f32),
            pltpu.VMEM((6, halves, rows, LANES), f32),
            pltpu.VMEM((6, ny, LANES), f32),
            pltpu.SemaphoreType.DMA((5, halves)),
            pltpu.SemaphoreType.DMA((10,)),
            pltpu.SemaphoreType.DMA((10,)),
        ],
        compiler_params=pltpu.CompilerParams(
            collective_id=0, has_side_effects=True, vmem_limit_bytes=40 * 2**20
        ),
    )(
        *[
            pltpu.with_memory_space_constraint(x.reshape(-1, nz), pltpu.HBM)
            for x in (density, velocity, pressure)
        ]
    )
    d, v, p = pl.pallas_call(
        functools.partial(z_kernel, planes, ny, halves),
        out_shape=[
            jax.ShapeDtypeStruct((rows, nz), f32),
            jax.ShapeDtypeStruct((3 * rows, nz), f32),
            jax.ShapeDtypeStruct((rows, nz), f32),
        ],
        in_specs=[vmem],
        out_specs=[vmem] * 3,
        scratch_shapes=[pltpu.VMEM((5, blocks * (LANES + 8), LANES), f32)],
        compiler_params=pltpu.CompilerParams(vmem_limit_bytes=40 * 2**20),
    )(turned)
    return d.reshape(density.shape), v.reshape(velocity.shape), p.reshape(density.shape)


def solution(mesh):
    field = P(None, "row", "col")
    vector = P(None, None, "row", "col")
    axes = (mesh.shape["row"], mesh.shape["col"])
    return jax.shard_map(
        functools.partial(on_device, axes),
        mesh=mesh,
        in_specs=(field, vector, field),
        out_specs=(field, vector, field),
        check_vma=False,
    )
```
